32 devices in a mesh: node: 2 (over x), row: 16 (over z, y, core).
Axes of the slice: x: 2, y: 2, z: 4, core: 2. Of those that a mesh axis runs over, the one named last changes fastest.
Arguments:
- hamiltonian: float32 [32, 7, 128, 128], P('row'), may hold values from -0.09375 to 0.09375
- column_blocks: int32 [32, 7], P('row'), may hold values from 0 to 31, as said below
- start_basis: float32 [4096, 256], P('row'), may hold values from -48 to 48
- node_re: float32 [6], P('node'), may hold values from 1.5 to 2.5
- node_im: float32 [6], P('node'), may hold values from 0.5 to 1.5
- weight_re: float32 [6], P('node'), may hold values from 0.5 to 1.5
- weight_im: float32 [6], P('node'), may hold values from -1 to 1
- sweep_count: int32 [6], P('node'), may hold values from 1 to 2, as said below
Outputs:
- basis: float32 [4096, 256], P('row')
The draws below stay inside these ranges and needn't reach their ends.
Inputs may be any that keep to these rules, and one draw needn't show every extreme that they name: `column_blocks`: tile 0 of row block b lies in column block b, tile 1 in b - 2 and tile 2 in b + 2, taken cyclically modulo 32; every other tile lies within 2 blocks of b, cyclically. `sweep_count`: some node takes 1 sweep and some node takes 2.
All inputs are finite; a program needn't handle non-finite values.
Results may differ from the reference program's by a relative error of at most 0.00022.
Values sent between devices are 32-bit elements; how exact they have to be, the bound alone decides.
No kernel may reach another device: no remote copies, remote signals or barrier semaphores. Data moves between devices by JAX's collectives and lax.ppermute only.
A program may use at most 64 MiB of HBM per device.

```python
import math
import jax
import jax.numpy as jnp
from jax import lax

TILE = 128
VECS = 256
BLOCK_NNZ = 7
REACH = 2
SWEEPS = 2
NS_ITERS = 2
NODES = 6
BLOCKS = 32
ROWS = 4096


def draw_column_blocks(key, part):
    positions = jnp.arange(BLOCKS, dtype=jnp.int32)
    extra = jax.random.randint(jax.random.fold_in(key, 11), (BLOCKS, BLOCK_NNZ - 3), -REACH, REACH + 1).astype(jnp.int32)
    fixed_part = jnp.broadcast_to(jnp.array([0, -REACH, REACH], jnp.int32), (BLOCKS, 3))
    offsets = jnp.concatenate([fixed_part, extra], axis=1)
    return ((positions[:, None] + offsets + BLOCKS) % BLOCKS).astype(jnp.int32)


def draw_start_basis(key, part):
    key_base = jax.random.fold_in(key, 21)
    key_cols = jax.random.fold_in(key, 22)
    positions = jnp.arange(ROWS, dtype=jnp.float32) / ROWS
    col_scale = jnp.exp(jax.random.uniform(key_cols, (VECS,), jnp.float32, 0.0, jnp.log(3.0)))
    base = jax.random.truncated_normal(key_base, -4.0, 4.0, (ROWS, VECS), jnp.float32)
    row_scale = jnp.exp(jnp.log(3.0) * positions)
    return (base * row_scale[:, None] * col_scale[None, :]).astype(jnp.float32)


def draw_sweep_count(key, part):
    counts = jax.random.randint(jax.random.fold_in(key, 31), (NODES,), 1, SWEEPS + 1).astype(jnp.int32)
    order = jax.random.permutation(jax.random.fold_in(key, 32), NODES)
    counts = counts.at[order[0]].set(1)
    counts = counts.at[order[1]].set(SWEEPS)
    return counts.astype(jnp.int32)


def steps_of(own_key, dims, cuts, smallest, top_value):
    level, own = 1.0, jax.random.fold_in(own_key, 6)
    for dim, parts in cuts:
        heights = jnp.exp(jax.random.uniform(jax.random.fold_in(own, dim), (parts,), jnp.float32, smallest / len(cuts), top_value / len(cuts)))
        level = level * jnp.repeat(heights, dims[dim] // parts).reshape([-1 if axis == dim else 1 for axis in range(len(dims))])
    return level


def noise(stream_key, dims, width, reach, shards=(), kind=jnp.bfloat16):
    result = jax.random.normal(stream_key, dims, jnp.float32) * width
    if len(shards) > 0:
        result = steps_of(stream_key, dims, shards, -0.22, 0.18) * result
    return jnp.clip(result, min=-reach, max=reach).astype(kind)


def setup_inputs(seed: int = 0) -> dict:
    key_list = jax.random.split(jax.random.key(seed), 9)
    return {
        "hamiltonian": noise(key_list[0], (BLOCKS, BLOCK_NNZ, TILE, TILE), (4 * BLOCK_NNZ * TILE) ** -0.5, 0.09375, ((0, 16),), jnp.float32),
        "column_blocks": draw_column_blocks(jax.random.fold_in(key_list[8], 71), 0),
        "start_basis": draw_start_basis(jax.random.fold_in(key_list[8], 71), 0),
        "node_re": jnp.clip(1.5 + 1.0 * jax.random.uniform(key_list[3], (NODES,), jnp.float32) ** steps_of(key_list[3], (NODES,), ((0, 2),), -0.2, 0.2), 1.5, 2.5),
        "node_im": jnp.clip(0.5 + 1.0 * jax.random.uniform(key_list[4], (NODES,), jnp.float32) ** steps_of(key_list[4], (NODES,), ((0, 2),), -0.2, 0.2), 0.5, 1.5),
        "weight_re": jnp.clip(0.5 + 1.0 * jax.random.uniform(key_list[5], (NODES,), jnp.float32) ** steps_of(key_list[5], (NODES,), ((0, 2),), -0.2, 0.2), 0.5, 1.5),
        "weight_im": jnp.clip(jax.random.uniform(key_list[6], (NODES,), jnp.float32, -1.0, 1.0) * steps_of(key_list[6], (NODES,), ((0, 2),), -0.4, 0.0), -1.0, 1.0),
        "sweep_count": draw_sweep_count(jax.random.fold_in(key_list[8], 71), 0),
    }


def apply_tiles(hamiltonian, column_blocks, vectors):
    breadth = vectors.shape[1]
    blocks = vectors.reshape(BLOCKS, TILE, breadth)
    summed = jnp.zeros((BLOCKS, TILE, breadth), jnp.float32)
    for column in range(BLOCK_NNZ):
        picked = jnp.take(blocks, column_blocks[:, column].astype(jnp.int32), axis=0)
        summed = summed + jnp.einsum('bij,bjw->biw', hamiltonian[:, column], picked, precision=lax.Precision.HIGHEST)
    return summed.reshape(BLOCKS * TILE, breadth)

def orthonormal(gram_matrix):
    norm_value = jnp.sqrt(jnp.sum(gram_matrix * gram_matrix) + 1e-06)
    matrix_a = gram_matrix / norm_value
    identity = jnp.eye(gram_matrix.shape[0], dtype=jnp.float32)
    current = identity
    for repeat in range(NS_ITERS):
        middle = 1.5 * identity - 0.5 * jnp.dot(current, matrix_a, precision=lax.Precision.HIGHEST)
        matrix_a = jnp.dot(matrix_a, middle, precision=lax.Precision.HIGHEST)
        current = jnp.dot(middle, current, precision=lax.Precision.HIGHEST)
    return (current, norm_value)

def reference(hamiltonian, column_blocks, start_basis, node_re, node_im, weight_re, weight_im, sweep_count):
    modulus = node_re * node_re + node_im * node_im
    inverse_re = node_re / modulus
    inverse_im = -node_im / modulus
    power_re, power_im = (inverse_re, inverse_im)
    krylov = start_basis
    filtered = jnp.zeros_like(start_basis)
    for degree in range(SWEEPS + 1):
        if degree > 0:
            krylov = apply_tiles(hamiltonian, column_blocks, krylov)
        active = (sweep_count >= degree).astype(jnp.float32)
        weight_sum = jnp.sum(active * (weight_re * power_re - weight_im * power_im))
        filtered = filtered + weight_sum * krylov
        power_re, power_im = (power_re * inverse_re - power_im * inverse_im, power_re * inverse_im + power_im * inverse_re)
    gram_matrix = lax.dot_general(filtered, filtered, (((0,), (0,)), ((), ())), precision=lax.Precision.HIGHEST)
    mixing, norm_value = orthonormal(gram_matrix)
    return math.sqrt(ROWS) * jnp.dot(filtered, mixing, precision=lax.Precision.HIGHEST) / jnp.sqrt(norm_value)
```

```python
import functools
import math

import jax
import jax.numpy as jnp
from jax import lax
from jax.experimental import pallas as pl
from jax.experimental.pallas import tpu as pltpu
from jax.sharding import PartitionSpec as P

SWEEPS = 2
Z_POLY = (2.25, -2.4375, 1.6875, -0.5625, 0.0625)
SUBLANES = 8

VMEM = pl.BlockSpec(memory_space=pltpu.VMEM)
SMEM = pl.BlockSpec(memory_space=pltpu.SMEM)


def split(x):
    high = x.astype(jnp.bfloat16)
    low = (x - high.astype(jnp.float32)).astype(jnp.bfloat16)
    return high, low


def mm(a, b, dims=((1,), (0,))):
    return lax.dot_general(a, b, (dims, ((), ())), preferred_element_type=jnp.float32)


def mm3(a_high, a_low, b_high, b_low):
    return mm(a_high, b_high) + (mm(a_high, b_low) + mm(a_low, b_high))


def prepare_kernel(total_blocks, cols_ref, ham_ref, high_ref, low_ref, odd_ref, wide):
    count_blocks, stored, tile, _ = ham_ref.shape
    first = cols_ref[0, 0]
    odd = (first // count_blocks) % 2
    odd_ref[...] = jnp.full(odd_ref.shape, odd, jnp.int32)
    wide[...] = jnp.zeros_like(wide)
    for block in range(count_blocks):
        for k in range(stored):
            away = lax.rem(cols_ref[block, k] - first + total_blocks, total_blocks)
            own = away < count_blocks
            right = jnp.logical_and(away >= count_blocks, away < 2 * count_blocks)
            within = jnp.where(
                own, away, jnp.where(right, away - count_blocks, away - total_blocks + count_blocks)
            )
            group = jnp.where(own, 0, jnp.where(right == (odd == 0), 1, 2))
            slot = group * count_blocks + within
            wide[block, slot] += ham_ref[block, k]
    for block in range(count_blocks):
        for slot in range(wide.shape[1]):
            high, low = split(wide[block, slot])
            rows = slice(block * tile, (block + 1) * tile)
            lanes = slice(slot * tile, (slot + 1) * tile)
            high_ref[rows, lanes] = high
            low_ref[rows, lanes] = low


def banded(high_ref, low_ref, parts):
    rows = parts[0].shape[0]
    total = None
    for index, part in enumerate(parts):
        lanes = slice(index * rows, (index + 1) * rows)
        b_high, b_low = split(part[...])
        term = mm3(high_ref[:, lanes], low_ref[:, lanes], b_high, b_low)
        total = term if total is None else total + term
    return total


def sweep_kernel(high_ref, low_ref, own_ref, core_ref, chip_ref, out_ref):
    out_ref[...] = banded(high_ref, low_ref, (own_ref, core_ref, chip_ref))


def gram_kernel(
    high_ref, low_ref, own_ref, core_ref, chip_ref, start_ref, coef_ref, other_ref, odd_ref,
    filtered_ref, mine_ref, theirs_ref,
):
    second = banded(high_ref, low_ref, (own_ref, core_ref, chip_ref))
    coef = coef_ref[...] + other_ref[...]
    filtered = (
        coef[0:1, 0:1] * start_ref[...] + coef[1:2, 0:1] * own_ref[...] + coef[2:3, 0:1] * second
    )
    filtered_ref[...] = filtered
    high, low = split(filtered)
    cross = mm(high, low, ((0,), (0,)))
    gram = mm(high, high, ((0,), (0,))) + (cross + cross.T)
    half = gram.shape[0] // 2
    row = lax.broadcasted_iota(jnp.int32, (half, half), 0)
    col = lax.broadcasted_iota(jnp.int32, (half, half), 1)
    upper, lower, side = gram[:half, :half], gram[half:, half:], gram[:half, half:]
    packed = jnp.where(col >= row, upper, lower)
    diagonal = jnp.sum(jnp.where(col == row, lower, 0.0), axis=0, keepdims=True)
    diagonal = jnp.broadcast_to(diagonal, (SUBLANES, half))
    odd = odd_ref[0:1, 0:1] == 1
    mine_ref[:half] = jnp.where(odd, packed, side)
    theirs_ref[:half] = jnp.where(odd, side, packed)
    mine_ref[half:] = diagonal
    theirs_ref[half:] = diagonal


def finish_kernel(row_scale, filtered_ref, mine_ref, theirs_ref, odd_ref, out_ref):
    half = mine_ref.shape[1]
    odd = odd_ref[0:1, 0:1] == 1
    mine, theirs = mine_ref[...], theirs_ref[...]
    packed = jnp.where(odd, mine, theirs)
    side = jnp.where(odd, theirs, mine)[:half]
    diagonal = packed[half:half + 1]
    packed = packed[:half]
    row = lax.broadcasted_iota(jnp.int32, (half, half), 0)
    col = lax.broadcasted_iota(jnp.int32, (half, half), 1)
    turned = packed.T
    upper = jnp.where(col >= row, packed, turned)
    lower = jnp.where(col < row, packed, jnp.where(col > row, turned, diagonal))
    gram = jnp.concatenate(
        [
            jnp.concatenate([upper, side], axis=1),
            jnp.concatenate([side.T, lower], axis=1),
        ],
        axis=0,
    )
    square = jnp.sum(jnp.sum(gram * gram, axis=0, keepdims=True), axis=1, keepdims=True)
    norm_value = jnp.sqrt(square + 1e-06)
    a = gram / norm_value
    a_high, a_low = split(a)
    a2 = mm3(a_high, a_low, a_high, a_low)
    b_high, b_low = split(a2)
    c_high, c_low = split(Z_POLY[3] * a + Z_POLY[4] * a2)
    rest = Z_POLY[1] * a + Z_POLY[2] * a2 + mm3(b_high, b_low, c_high, c_low)
    z_high, z_low = split(rest)
    filtered = filtered_ref[...]
    f_high, f_low = split(filtered)
    scale = row_scale / jnp.sqrt(norm_value)
    out_ref[...] = scale * (Z_POLY[0] * filtered + mm3(f_high, f_low, z_high, z_low))


def call(kernel, out_shape, n_in, smem=(), scratch=(), flops=0, moved=0, name=None):
    n_out = len(out_shape) if isinstance(out_shape, (tuple, list)) else 1
    return pl.pallas_call(
        kernel,
        out_shape=out_shape,
        in_specs=[SMEM if i in smem else VMEM for i in range(n_in)],
        out_specs=[VMEM] * n_out if isinstance(out_shape, (tuple, list)) else VMEM,
        scratch_shapes=scratch,
        cost_estimate=pl.CostEstimate(flops=flops, bytes_accessed=moved, transcendentals=0),
        compiler_params=pltpu.CompilerParams(vmem_limit_bytes=24 * 2**20),
        name=name,
    )


def on_device(
    hamiltonian, column_blocks, start_basis, node_re, node_im, weight_re, weight_im, sweep_count
):
    f32 = jnp.float32
    count_blocks, stored, tile, _ = hamiltonian.shape
    rows, vecs = start_basis.shape
    devices = lax.axis_size("row")
    nodes = lax.axis_size("node")
    row_scale = math.sqrt(rows * devices)

    core_pairs = [(i, i ^ 1) for i in range(devices)]
    chip_pairs = [(i, (i + (1 if i % 2 else -1)) % devices) for i in range(devices)]

    def halo(block):
        chip = lax.ppermute(block, "row", chip_pairs)
        core = lax.ppermute(block, "row", core_pairs)
        return core, chip

    modulus = node_re * node_re + node_im * node_im
    inverse_re = node_re / modulus
    inverse_im = -node_im / modulus
    power_re, power_im = inverse_re, inverse_im
    listed = []
    for degree in range(SWEEPS + 1):
        active = (sweep_count >= degree).astype(f32)
        listed.append(jnp.sum(active * (weight_re * power_re - weight_im * power_im)))
        power_re, power_im = (
            power_re * inverse_re - power_im * inverse_im,
            power_re * inverse_im + power_im * inverse_re,
        )
    listed += [jnp.zeros((), f32)] * (SUBLANES - len(listed))
    coef = jnp.broadcast_to(jnp.stack(listed)[:, None], (SUBLANES, 128))

    start_core, start_chip = halo(start_basis)
    wide = rows * 3
    high, low, odd = call(
        functools.partial(prepare_kernel, count_blocks * devices),
        (
            jax.ShapeDtypeStruct((rows, wide), jnp.bfloat16),
            jax.ShapeDtypeStruct((rows, wide), jnp.bfloat16),
            jax.ShapeDtypeStruct((SUBLANES, 128), jnp.int32),
        ),
        2,
        smem=(0,),
        scratch=[pltpu.VMEM((count_blocks, 3 * count_blocks, tile, tile), f32)],
        flops=hamiltonian.size * 4,
        moved=hamiltonian.size * 4 + rows * wide * 8,
        name="prepare",
    )(column_blocks, hamiltonian)

    other = coef
    for shift in range(1, nodes):
        moved = lax.ppermute(coef, "node", [(i, i ^ shift) for i in range(nodes)])
        other = moved if shift == 1 else other + moved

    first = call(
        sweep_kernel,
        jax.ShapeDtypeStruct((rows, vecs), f32),
        5,
        flops=6 * rows * wide * vecs,
        moved=rows * wide * 4 + 16 * rows * vecs,
        name="sweep",
    )(high, low, start_basis, start_core, start_chip)
    first_core, first_chip = halo(first)

    half = vecs // 2
    part = jax.ShapeDtypeStruct((half + SUBLANES, half), f32)
    filtered, mine, theirs = call(
        gram_kernel,
        (jax.ShapeDtypeStruct((rows, vecs), f32), part, part),
        9,
        flops=6 * rows * wide * vecs + 4 * rows * vecs * vecs,
        moved=rows * wide * 4 + 20 * rows * vecs,
        name="gram",
    )(high, low, first, first_core, first_chip, start_basis, coef, other, odd)

    total = mine + lax.ppermute(theirs, "row", core_pairs)
    step = 2
    while step < devices:
        total = total + lax.ppermute(total, "row", [(i, i ^ step) for i in range(devices)])
        step *= 2
    theirs = lax.ppermute(total, "row", core_pairs)

    return call(
        functools.partial(finish_kernel, row_scale),
        jax.ShapeDtypeStruct((rows, vecs), f32),
        4,
        flops=18 * vecs**3,
        moved=8 * rows * vecs + 4 * vecs * vecs,
        name="finish",
    )(filtered, total, theirs, odd)


def solution(mesh):
    return jax.shard_map(
        on_device,
        mesh=mesh,
        in_specs=(
            P("row", None, None, None),
            P("row", None),
            P("row", None),
            P("node"),
            P("node"),
            P("node"),
            P("node"),
            P("node"),
        ),
        out_specs=P("row", None),
        check_vma=False,
    )
```

```python
import functools
import math

import jax
import jax.numpy as jnp
from jax import lax
from jax.experimental import pallas as pl
from jax.experimental.pallas import tpu as pltpu
from jax.sharding import PartitionSpec as P

SWEEPS = 2
Z_POLY = (2.25, -2.4375, 1.6875, -0.5625, 0.0625)
SUBLANES = 8

VMEM = pl.BlockSpec(memory_space=pltpu.VMEM)
SMEM = pl.BlockSpec(memory_space=pltpu.SMEM)


def split(x):
    high = x.astype(jnp.bfloat16)
    low = (x - high.astype(jnp.float32)).astype(jnp.bfloat16)
    return high, low


def mm(a, b, dims=((1,), (0,))):
    return lax.dot_general(a, b, (dims, ((), ())), preferred_element_type=jnp.float32)


def mm3(a_high, a_low, b_high, b_low):
    return mm(a_high, b_high) + (mm(a_high, b_low) + mm(a_low, b_high))


def prepare_kernel(total_blocks, cols_ref, *refs):
    shares, (ham_ref, high_ref, low_ref, odd_ref, coef_ref, wide) = refs[:-6], refs[-6:]
    row = lax.broadcasted_iota(jnp.int32, coef_ref.shape, 0)
    coef = jnp.zeros(coef_ref.shape, jnp.float32)
    for degree, share in enumerate(shares):
        coef = jnp.where(row == degree, jnp.sum(share[...], axis=1, keepdims=True), coef)
    coef_ref[...] = coef
    count_blocks, stored, tile, _ = ham_ref.shape
    first = cols_ref[0, 0]
    odd = (first // count_blocks) % 2
    odd_ref[...] = jnp.full(odd_ref.shape, odd, jnp.int32)
    wide[...] = jnp.zeros_like(wide)
    for block in range(count_blocks):
        for k in range(stored):
            away = lax.rem(cols_ref[block, k] - first + total_blocks, total_blocks)
            own = away < count_blocks
            right = jnp.logical_and(away >= count_blocks, away < 2 * count_blocks)
            within = jnp.where(
                own, away, jnp.where(right, away - count_blocks, away - total_blocks + count_blocks)
            )
            group = jnp.where(own, 0, jnp.where(right == (odd == 0), 1, 2))
            slot = group * count_blocks + within
            wide[block, slot] += ham_ref[block, k]
    for block in range(count_blocks):
        for slot in range(wide.shape[1]):
            high, low = split(wide[block, slot])
            rows = slice(block * tile, (block + 1) * tile)
            lanes = slice(slot * tile, (slot + 1) * tile)
            high_ref[rows, lanes] = high
            low_ref[rows, lanes] = low


def banded(high_ref, low_ref, parts):
    rows = parts[0].shape[0]
    total = None
    for index, part in enumerate(parts):
        lanes = slice(index * rows, (index + 1) * rows)
        b_high, b_low = split(part[...])
        term = mm3(high_ref[:, lanes], low_ref[:, lanes], b_high, b_low)
        total = term if total is None else total + term
    return total


def sweep_kernel(high_ref, low_ref, own_ref, core_ref, chip_ref, out_ref):
    out_ref[...] = banded(high_ref, low_ref, (own_ref, core_ref, chip_ref))


def gram_kernel(
    high_ref, low_ref, own_ref, core_ref, chip_ref, start_ref, coef_ref, other_ref, odd_ref,
    filtered_ref, mine_ref, theirs_ref,
):
    second = banded(high_ref, low_ref, (own_ref, core_ref, chip_ref))
    coef = coef_ref[...] + other_ref[...]
    filtered = (
        coef[0:1, 0:1] * start_ref[...] + coef[1:2, 0:1] * own_ref[...] + coef[2:3, 0:1] * second
    )
    filtered_ref[...] = filtered
    high, low = split(filtered)
    cross = mm(high, low, ((0,), (0,)))
    gram = mm(high, high, ((0,), (0,))) + (cross + cross.T)
    half = gram.shape[0] // 2
    row = lax.broadcasted_iota(jnp.int32, (half, half), 0)
    col = lax.broadcasted_iota(jnp.int32, (half, half), 1)
    upper, lower, side = gram[:half, :half], gram[half:, half:], gram[:half, half:]
    packed = jnp.where(col >= row, upper, lower)
    diagonal = jnp.sum(jnp.where(col == row, lower, 0.0), axis=0, keepdims=True)
    diagonal = jnp.broadcast_to(diagonal, (SUBLANES, half))
    odd = odd_ref[0:1, 0:1] == 1
    mine_ref[:half] = jnp.where(odd, packed, side)
    theirs_ref[:half] = jnp.where(odd, side, packed)
    mine_ref[half:] = diagonal
    theirs_ref[half:] = diagonal


def finish_kernel(row_scale, filtered_ref, mine_ref, theirs_ref, odd_ref, out_ref):
    half = mine_ref.shape[1]
    odd = odd_ref[0:1, 0:1] == 1
    mine, theirs = mine_ref[...], theirs_ref[...]
    packed = jnp.where(odd, mine, theirs)
    side = jnp.where(odd, theirs, mine)[:half]
    diagonal = packed[half:half + 1]
    packed = packed[:half]
    row = lax.broadcasted_iota(jnp.int32, (half, half), 0)
    col = lax.broadcasted_iota(jnp.int32, (half, half), 1)
    turned = packed.T
    upper = jnp.where(col >= row, packed, turned)
    lower = jnp.where(col < row, packed, jnp.where(col > row, turned, diagonal))
    gram = jnp.concatenate(
        [
            jnp.concatenate([upper, side], axis=1),
            jnp.concatenate([side.T, lower], axis=1),
        ],
        axis=0,
    )
    square = jnp.sum(jnp.sum(gram * gram, axis=0, keepdims=True), axis=1, keepdims=True)
    norm_value = jnp.sqrt(square + 1e-06)
    a = gram / norm_value
    a_high, a_low = split(a)
    a2 = mm3(a_high, a_low, a_high, a_low)
    b_high, b_low = split(a2)
    c_high, c_low = split(Z_POLY[3] * a + Z_POLY[4] * a2)
    rest = Z_POLY[1] * a + Z_POLY[2] * a2 + mm3(b_high, b_low, c_high, c_low)
    z_high, z_low = split(rest)
    filtered = filtered_ref[...]
    f_high, f_low = split(filtered)
    scale = row_scale / jnp.sqrt(norm_value)
    out_ref[...] = scale * (Z_POLY[0] * filtered + mm3(f_high, f_low, z_high, z_low))


def call(kernel, out_shape, n_in, smem=(), scratch=(), flops=0, moved=0, name=None):
    n_out = len(out_shape) if isinstance(out_shape, (tuple, list)) else 1
    return pl.pallas_call(
        kernel,
        out_shape=out_shape,
        in_specs=[SMEM if i in smem else VMEM for i in range(n_in)],
        out_specs=[VMEM] * n_out if isinstance(out_shape, (tuple, list)) else VMEM,
        scratch_shapes=scratch,
        cost_estimate=pl.CostEstimate(flops=flops, bytes_accessed=moved, transcendentals=0),
        compiler_params=pltpu.CompilerParams(vmem_limit_bytes=24 * 2**20),
        name=name,
    )


def on_device(
    hamiltonian, column_blocks, start_basis, node_re, node_im, weight_re, weight_im, sweep_count
):
    f32 = jnp.float32
    count_blocks, stored, tile, _ = hamiltonian.shape
    rows, vecs = start_basis.shape
    devices = lax.axis_size("row")
    nodes = lax.axis_size("node")
    row_scale = math.sqrt(rows * devices)

    core_pairs = [(i, i ^ 1) for i in range(devices)]
    chip_pairs = [(i, (i + (1 if i % 2 else -1)) % devices) for i in range(devices)]

    def halo(block):
        chip = lax.ppermute(block, "row", chip_pairs)
        core = lax.ppermute(block, "row", core_pairs)
        return core, chip

    modulus = node_re * node_re + node_im * node_im
    inverse_re = node_re / modulus
    inverse_im = -node_im / modulus
    power_re, power_im = inverse_re, inverse_im
    listed = []
    for degree in range(SWEEPS + 1):
        active = (sweep_count >= degree).astype(f32)
        listed.append((active * (weight_re * power_re - weight_im * power_im))[None, :])
        power_re, power_im = (
            power_re * inverse_re - power_im * inverse_im,
            power_re * inverse_im + power_im * inverse_re,
        )
    start_core, start_chip = halo(start_basis)
    wide = rows * 3
    high, low, odd, coef = call(
        functools.partial(prepare_kernel, count_blocks * devices),
        (
            jax.ShapeDtypeStruct((rows, wide), jnp.bfloat16),
            jax.ShapeDtypeStruct((rows, wide), jnp.bfloat16),
            jax.ShapeDtypeStruct((SUBLANES, 128), jnp.int32),
            jax.ShapeDtypeStruct((SUBLANES, 128), f32),
        ),
        2 + len(listed),
        smem=(0,),
        scratch=[pltpu.VMEM((count_blocks, 3 * count_blocks, tile, tile), f32)],
        flops=hamiltonian.size * 4,
        moved=hamiltonian.size * 4 + rows * wide * 8,
        name="prepare",
    )(column_blocks, *listed, hamiltonian)

    first = call(
        sweep_kernel,
        jax.ShapeDtypeStruct((rows, vecs), f32),
        5,
        flops=6 * rows * wide * vecs,
        moved=rows * wide * 4 + 16 * rows * vecs,
        name="sweep",
    )(high, low, start_basis, start_core, start_chip)
    first, coef = lax.optimization_barrier((first, coef))
    first_core, first_chip = halo(first)
    other = coef
    for shift in range(1, nodes):
        moved = lax.ppermute(coef, "node", [(i, i ^ shift) for i in range(nodes)])
        other = moved if shift == 1 else other + moved

    half = vecs // 2
    part = jax.ShapeDtypeStruct((half + SUBLANES, half), f32)
    filtered, mine, theirs = call(
        gram_kernel,
        (jax.ShapeDtypeStruct((rows, vecs), f32), part, part),
        9,
        flops=6 * rows * wide * vecs + 4 * rows * vecs * vecs,
        moved=rows * wide * 4 + 20 * rows * vecs,
        name="gram",
    )(high, low, first, first_core, first_chip, start_basis, coef, other, odd)

    total = mine + lax.ppermute(theirs, "row", core_pairs)
    step = 2
    while step < devices:
        total = total + lax.ppermute(total, "row", [(i, i ^ step) for i in range(devices)])
        step *= 2
    theirs = lax.ppermute(total, "row", core_pairs)

    return call(
        functools.partial(finish_kernel, row_scale),
        jax.ShapeDtypeStruct((rows, vecs), f32),
        4,
        flops=18 * vecs**3,
        moved=8 * rows * vecs + 4 * vecs * vecs,
        name="finish",
    )(filtered, total, theirs, odd)


def solution(mesh):
    return jax.shard_map(
        on_device,
        mesh=mesh,
        in_specs=(
            P("row", None, None, None),
            P("row", None),
            P("row", None),
            P("node"),
            P("node"),
            P("node"),
            P("node"),
            P("node"),
        ),
        out_specs=P("row", None),
        check_vma=False,
    )
```

```python
import functools
import math

import jax
import jax.numpy as jnp
from jax import lax
from jax.experimental import pallas as pl
from jax.experimental.pallas import tpu as pltpu
from jax.sharding import PartitionSpec as P

SWEEPS = 2
Z_POLY = (2.25, -2.4375, 1.6875, -0.5625, 0.0625)
SUBLANES = 8

VMEM = pl.BlockSpec(memory_space=pltpu.VMEM)
SMEM = pl.BlockSpec(memory_space=pltpu.SMEM)


def split(x):
    high = x.astype(jnp.bfloat16)
    low = (x - high.astype(jnp.float32)).astype(jnp.bfloat16)
    return high, low


def mm(a, b, dims=((1,), (0,))):
    return lax.dot_general(a, b, (dims, ((), ())), preferred_element_type=jnp.float32)


def mm3(a_high, a_low, b_high, b_low):
    return mm(a_high, b_high) + (mm(a_high, b_low) + mm(a_low, b_high))


def prepare_kernel(total_blocks, cols_ref, *refs):
    shares, (ham_ref, high_ref, low_ref, odd_ref, coef_ref, wide) = refs[:-6], refs[-6:]
    row = lax.broadcasted_iota(jnp.int32, coef_ref.shape, 0)
    coef = jnp.zeros(coef_ref.shape, jnp.float32)
    for degree, share in enumerate(shares):
        coef = jnp.where(row == degree, jnp.sum(share[...], axis=1, keepdims=True), coef)
    coef_ref[...] = coef
    count_blocks, stored, tile, _ = ham_ref.shape
    first = cols_ref[0, 0]
    odd = (first // count_blocks) % 2
    odd_ref[...] = jnp.full(odd_ref.shape, odd, jnp.int32)
    wide[...] = jnp.zeros_like(wide)
    for block in range(count_blocks):
        for k in range(stored):
            away = lax.rem(cols_ref[block, k] - first + total_blocks, total_blocks)
            own = away < count_blocks
            right = jnp.logical_and(away >= count_blocks, away < 2 * count_blocks)
            within = jnp.where(
                own, away, jnp.where(right, away - count_blocks, away - total_blocks + count_blocks)
            )
            group = jnp.where(own, 0, jnp.where(right == (odd == 0), 1, 2))
            slot = group * count_blocks + within
            wide[block, slot] += ham_ref[block, k]
    for block in range(count_blocks):
        for slot in range(wide.shape[1]):
            high, low = split(wide[block, slot])
            rows = slice(block * tile, (block + 1) * tile)
            lanes = slice(slot * tile, (slot + 1) * tile)
            high_ref[rows, lanes] = high
            low_ref[rows, lanes] = low


def banded(high_ref, low_ref, parts):
    rows = parts[0].shape[0]
    total = None
    for index, part in enumerate(parts):
        lanes = slice(index * rows, (index + 1) * rows)
        b_high, b_low = split(part[...])
        term = mm3(high_ref[:, lanes], low_ref[:, lanes], b_high, b_low)
        total = term if total is None else total + term
    return total


def sweep_kernel(high_ref, low_ref, own_ref, core_ref, chip_ref, out_ref):
    out_ref[...] = banded(high_ref, low_ref, (own_ref, core_ref, chip_ref))


def gram_kernel(
    high_ref, low_ref, own_ref, core_ref, chip_ref, start_ref, coef_ref, other_ref, odd_ref,
    filtered_ref, mine_ref, theirs_ref,
):
    second = banded(high_ref, low_ref, (own_ref, core_ref, chip_ref))
    coef = coef_ref[...] + other_ref[...]
    filtered = (
        coef[0:1, 0:1] * start_ref[...] + coef[1:2, 0:1] * own_ref[...] + coef[2:3, 0:1] * second
    )
    filtered_ref[...] = filtered
    high, low = split(filtered)
    cross = mm(high, low, ((0,), (0,)))
    gram = mm(high, high, ((0,), (0,))) + (cross + cross.T)
    half = gram.shape[0] // 2
    row = lax.broadcasted_iota(jnp.int32, (half, half), 0)
    col = lax.broadcasted_iota(jnp.int32, (half, half), 1)
    upper, lower, side = gram[:half, :half], gram[half:, half:], gram[:half, half:]
    packed = jnp.where(col >= row, upper, lower)
    diagonal = jnp.sum(jnp.where(col == row, lower, 0.0), axis=0, keepdims=True)
    diagonal = jnp.broadcast_to(diagonal, (SUBLANES, half))
    odd = odd_ref[0:1, 0:1] == 1
    mine_ref[:half] = jnp.where(odd, packed, side)
    theirs_ref[:half] = jnp.where(odd, side, packed)
    mine_ref[half:] = diagonal
    theirs_ref[half:] = diagonal


def finish_kernel(row_scale, filtered_ref, mine_ref, theirs_ref, odd_ref, out_ref):
    half = mine_ref.shape[1]
    odd = odd_ref[0:1, 0:1] == 1
    mine, theirs = mine_ref[...], theirs_ref[...]
    packed = jnp.where(odd, mine, theirs)
    side = jnp.where(odd, theirs, mine)[:half]
    diagonal = packed[half:half + 1]
    packed = packed[:half]
    row = lax.broadcasted_iota(jnp.int32, (half, half), 0)
    col = lax.broadcasted_iota(jnp.int32, (half, half), 1)
    turned = packed.T
    upper = jnp.where(col >= row, packed, turned)
    lower = jnp.where(col < row, packed, jnp.where(col > row, turned, diagonal))
    gram = jnp.concatenate(
        [
            jnp.concatenate([upper, side], axis=1),
            jnp.concatenate([side.T, lower], axis=1),
        ],
        axis=0,
    )
    square = jnp.sum(jnp.sum(gram * gram, axis=0, keepdims=True), axis=1, keepdims=True)
    norm_value = jnp.sqrt(square + 1e-06)
    a = gram / norm_value
    a_high, a_low = split(a)
    a2 = mm3(a_high, a_low, a_high, a_low)
    b_high, b_low = split(a2)
    c_high, c_low = split(Z_POLY[3] * a + Z_POLY[4] * a2)
    rest = Z_POLY[1] * a + Z_POLY[2] * a2 + mm3(b_high, b_low, c_high, c_low)
    z_high, z_low = split(rest)
    filtered = filtered_ref[...]
    f_high, f_low = split(filtered)
    scale = row_scale / jnp.sqrt(norm_value)
    out_ref[...] = scale * (Z_POLY[0] * filtered + mm3(f_high, f_low, z_high, z_low))


def sum_up(total, moved):
    total = total + moved[0]
    if len(moved) == 3:
        total = total + (moved[1] + moved[2])
    return total


def call(kernel, out_shape, n_in, smem=(), scratch=(), flops=0, moved=0, name=None):
    n_out = len(out_shape) if isinstance(out_shape, (tuple, list)) else 1
    return pl.pallas_call(
        kernel,
        out_shape=out_shape,
        in_specs=[SMEM if i in smem else VMEM for i in range(n_in)],
        out_specs=[VMEM] * n_out if isinstance(out_shape, (tuple, list)) else VMEM,
        scratch_shapes=scratch,
        cost_estimate=pl.CostEstimate(flops=flops, bytes_accessed=moved, transcendentals=0),
        compiler_params=pltpu.CompilerParams(vmem_limit_bytes=24 * 2**20),
        name=name,
    )


def on_device(
    hamiltonian, column_blocks, start_basis, node_re, node_im, weight_re, weight_im, sweep_count
):
    f32 = jnp.float32
    count_blocks, stored, tile, _ = hamiltonian.shape
    rows, vecs = start_basis.shape
    devices = lax.axis_size("row")
    nodes = lax.axis_size("node")
    row_scale = math.sqrt(rows * devices)

    core_pairs = [(i, i ^ 1) for i in range(devices)]
    chip_pairs = [(i, (i + (1 if i % 2 else -1)) % devices) for i in range(devices)]

    def halo(block):
        chip = lax.ppermute(block, "row", chip_pairs)
        core = lax.ppermute(block, "row", core_pairs)
        return core, chip

    modulus = node_re * node_re + node_im * node_im
    inverse_re = node_re / modulus
    inverse_im = -node_im / modulus
    power_re, power_im = inverse_re, inverse_im
    listed = []
    for degree in range(SWEEPS + 1):
        active = (sweep_count >= degree).astype(f32)
        listed.append((active * (weight_re * power_re - weight_im * power_im))[None, :])
        power_re, power_im = (
            power_re * inverse_re - power_im * inverse_im,
            power_re * inverse_im + power_im * inverse_re,
        )
    start_core, start_chip = halo(start_basis)
    wide = rows * 3
    high, low, odd, coef = call(
        functools.partial(prepare_kernel, count_blocks * devices),
        (
            jax.ShapeDtypeStruct((rows, wide), jnp.bfloat16),
            jax.ShapeDtypeStruct((rows, wide), jnp.bfloat16),
            jax.ShapeDtypeStruct((SUBLANES, 128), jnp.int32),
            jax.ShapeDtypeStruct((SUBLANES, 128), f32),
        ),
        2 + len(listed),
        smem=(0,),
        scratch=[pltpu.VMEM((count_blocks, 3 * count_blocks, tile, tile), f32)],
        flops=hamiltonian.size * 4,
        moved=hamiltonian.size * 4 + rows * wide * 8,
        name="prepare",
    )(column_blocks, *listed, hamiltonian)

    first = call(
        sweep_kernel,
        jax.ShapeDtypeStruct((rows, vecs), f32),
        5,
        flops=6 * rows * wide * vecs,
        moved=rows * wide * 4 + 16 * rows * vecs,
        name="sweep",
    )(high, low, start_basis, start_core, start_chip)
    first, coef = lax.optimization_barrier((first, coef))
    first_core, first_chip = halo(first)
    other = coef
    for shift in range(1, nodes):
        moved = lax.ppermute(coef, "node", [(i, i ^ shift) for i in range(nodes)])
        other = moved if shift == 1 else other + moved

    half = vecs // 2
    part = jax.ShapeDtypeStruct((half + SUBLANES, half), f32)
    filtered, mine, theirs = call(
        gram_kernel,
        (jax.ShapeDtypeStruct((rows, vecs), f32), part, part),
        9,
        flops=6 * rows * wide * vecs + 4 * rows * vecs * vecs,
        moved=rows * wide * 4 + 20 * rows * vecs,
        name="gram",
    )(high, low, first, first_core, first_chip, start_basis, coef, other, odd)

    total = mine + lax.ppermute(theirs, "row", core_pairs)
    steps = [1 << bit for bit in range(1, (devices - 1).bit_length())]
    phases = [[steps[0], steps[1], steps[0] + steps[1]]] if len(steps) > 1 else [steps]
    for phase in phases + [[step] for step in steps[2:]]:
        moved = [
            lax.ppermute(total, "row", [(i, i ^ step) for i in range(devices)]) for step in phase
        ]
        total = sum_up(total, moved)
    theirs = lax.ppermute(total, "row", core_pairs)

    return call(
        functools.partial(finish_kernel, row_scale),
        jax.ShapeDtypeStruct((rows, vecs), f32),
        4,
        flops=18 * vecs**3,
        moved=8 * rows * vecs + 4 * vecs * vecs,
        name="finish",
    )(filtered, total, theirs, odd)


def solution(mesh):
    return jax.shard_map(
        on_device,
        mesh=mesh,
        in_specs=(
            P("row", None, None, None),
            P("row", None),
            P("row", None),
            P("node"),
            P("node"),
            P("node"),
            P("node"),
            P("node"),
        ),
        out_specs=P("row", None),
        check_vma=False,
    )
```

```python
import functools
import math

import jax
import jax.numpy as jnp
from jax import lax
from jax.experimental import pallas as pl
from jax.experimental.pallas import tpu as pltpu
from jax.sharding import PartitionSpec as P

SWEEPS = 2
Z_POLY = (2.25, -2.4375, 1.6875, -0.5625, 0.0625)
SUBLANES = 8

VMEM = pl.BlockSpec(memory_space=pltpu.VMEM)
ANY = pl.BlockSpec(memory_space=pl.ANY)
SMEM = pl.BlockSpec(memory_space=pltpu.SMEM)


def split(x):
    high = x.astype(jnp.bfloat16)
    low = (x - high.astype(jnp.float32)).astype(jnp.bfloat16)
    return high, low


def mm(a, b, dims=((1,), (0,))):
    return lax.dot_general(a, b, (dims, ((), ())), preferred_element_type=jnp.float32)


def mm3(a_high, a_low, b_high, b_low):
    return mm(a_high, b_high) + (mm(a_high, b_low) + mm(a_low, b_high))


def prepare_kernel(total_blocks, cols_ref, *refs):
    shares, (ham_ref, high_ref, low_ref, odd_ref, coef_ref, wide) = refs[:-6], refs[-6:]
    row = lax.broadcasted_iota(jnp.int32, coef_ref.shape, 0)
    coef = jnp.zeros(coef_ref.shape, jnp.float32)
    for degree, share in enumerate(shares):
        coef = jnp.where(row == degree, jnp.sum(share[...], axis=1, keepdims=True), coef)
    coef_ref[...] = coef
    count_blocks, stored, tile, _ = ham_ref.shape
    first = cols_ref[0, 0]
    odd = (first // count_blocks) % 2
    odd_ref[...] = jnp.full(odd_ref.shape, odd, jnp.int32)
    wide[...] = jnp.zeros_like(wide)
    for block in range(count_blocks):
        for k in range(stored):
            away = lax.rem(cols_ref[block, k] - first + total_blocks, total_blocks)
            own = away < count_blocks
            right = jnp.logical_and(away >= count_blocks, away < 2 * count_blocks)
            within = jnp.where(
                own, away, jnp.where(right, away - count_blocks, away - total_blocks + count_blocks)
            )
            group = jnp.where(own, 0, jnp.where(right == (odd == 0), 1, 2))
            slot = group * count_blocks + within
            wide[block, slot] += ham_ref[block, k]
    for block in range(count_blocks):
        for slot in range(wide.shape[1]):
            high, low = split(wide[block, slot])
            rows = slice(block * tile, (block + 1) * tile)
            lanes = slice(slot * tile, (slot + 1) * tile)
            high_ref[rows, lanes] = high
            low_ref[rows, lanes] = low


def banded(high_ref, low_ref, first, parts):
    rows = parts[0].shape[0]
    total = None
    for index, part in enumerate(parts, first):
        lanes = slice(index * rows, (index + 1) * rows)
        b_high, b_low = split(part[...])
        term = mm3(high_ref[:, lanes], low_ref[:, lanes], b_high, b_low)
        total = term if total is None else total + term
    return total


def near_kernel(high_ref, low_ref, own_ref, out_ref):
    out_ref[...] = banded(high_ref, low_ref, 0, (own_ref,))


def sweep_kernel(high_ref, low_ref, own_ref, core_ref, chip_ref, out_ref):
    out_ref[...] = banded(high_ref, low_ref, 0, (own_ref, core_ref, chip_ref))


def gram_kernel(
    high_ref, low_ref, own_ref, near_ref, core_ref, chip_ref, start_ref, coef_ref, other_ref, odd_ref,
    filtered_ref, mine_ref, theirs_ref,
):
    second = near_ref[...] + banded(high_ref, low_ref, 1, (core_ref, chip_ref))
    coef = coef_ref[...] + other_ref[...]
    filtered = (
        coef[0:1, 0:1] * start_ref[...] + coef[1:2, 0:1] * own_ref[...] + coef[2:3, 0:1] * second
    )
    filtered_ref[...] = filtered
    high, low = split(filtered)
    cross = mm(high, low, ((0,), (0,)))
    gram = mm(high, high, ((0,), (0,))) + (cross + cross.T)
    half = gram.shape[0] // 2
    row = lax.broadcasted_iota(jnp.int32, (half, half), 0)
    col = lax.broadcasted_iota(jnp.int32, (half, half), 1)
    upper, lower, side = gram[:half, :half], gram[half:, half:], gram[:half, half:]
    packed = jnp.where(col >= row, upper, lower)
    diagonal = jnp.sum(jnp.where(col == row, lower, 0.0), axis=0, keepdims=True)
    diagonal = jnp.broadcast_to(diagonal, (SUBLANES, half))
    odd = odd_ref[0:1, 0:1] == 1
    mine_ref[:half] = jnp.where(odd, packed, side)
    theirs_ref[:half] = jnp.where(odd, side, packed)
    mine_ref[half:] = diagonal
    theirs_ref[half:] = diagonal


def finish_kernel(row_scale, filtered_ref, mine_ref, theirs_ref, odd_ref, out_ref, held, sems):
    half = mine_ref.shape[1]
    odd = odd_ref[0:1, 0:1] == 1
    mine, theirs = mine_ref[...], theirs_ref[...]
    packed = jnp.where(odd, mine, theirs)
    side = jnp.where(odd, theirs, mine)[:half]
    diagonal = packed[half:half + 1]
    packed = packed[:half]
    row = lax.broadcasted_iota(jnp.int32, (half, half), 0)
    col = lax.broadcasted_iota(jnp.int32, (half, half), 1)
    turned = packed.T
    upper = jnp.where(col >= row, packed, turned)
    lower = jnp.where(col < row, packed, jnp.where(col > row, turned, diagonal))
    gram = jnp.concatenate(
        [
            jnp.concatenate([upper, side], axis=1),
            jnp.concatenate([side.T, lower], axis=1),
        ],
        axis=0,
    )
    g_high, g_low = split(gram)
    gram2 = mm3(g_high, g_low, g_high, g_low)
    squares = upper * upper + lower * lower + 2.0 * (side * side)
    square = jnp.sum(jnp.sum(squares, axis=0, keepdims=True), axis=1, keepdims=True)
    norm_value = jnp.sqrt(square + 1e-06)
    inverse = 1.0 / norm_value
    a = gram * inverse
    a2 = (gram2 * inverse) * inverse
    b_high, b_low = split(a2)
    c_high, c_low = split(Z_POLY[3] * a + Z_POLY[4] * a2)
    rest = Z_POLY[1] * a + Z_POLY[2] * a2 + mm3(b_high, b_low, c_high, c_low)
    scale = row_scale / jnp.sqrt(norm_value)
    z_high, z_low = split(rest)
    pieces = sems.shape[0]
    rows = out_ref.shape[0] // pieces
    copies = []
    for piece in range(pieces):
        part = pl.ds(piece * rows, rows)
        filtered = filtered_ref[part, :]
        f_high, f_low = split(filtered)
        held[part, :] = scale * (Z_POLY[0] * filtered + mm3(f_high, f_low, z_high, z_low))
        copy = pltpu.make_async_copy(held.at[part, :], out_ref.at[part, :], sems.at[piece])
        copy.start()
        copies.append(copy)
    for copy in copies:
        copy.wait()


def sum_up(total, moved):
    total = total + moved[0]
    if len(moved) == 3:
        total = total + (moved[1] + moved[2])
    return total


def call(kernel, out_shape, n_in, smem=(), out_any=False, scratch=(), flops=0, moved=0, name=None):
    n_out = len(out_shape) if isinstance(out_shape, (tuple, list)) else 1
    return pl.pallas_call(
        kernel,
        out_shape=out_shape,
        in_specs=[SMEM if i in smem else VMEM for i in range(n_in)],
        out_specs=[VMEM] * n_out if isinstance(out_shape, (tuple, list)) else ANY if out_any else VMEM,
        scratch_shapes=scratch,
        cost_estimate=pl.CostEstimate(flops=flops, bytes_accessed=moved, transcendentals=0),
        compiler_params=pltpu.CompilerParams(vmem_limit_bytes=24 * 2**20),
        name=name,
    )


def on_device(
    hamiltonian, column_blocks, start_basis, node_re, node_im, weight_re, weight_im, sweep_count
):
    f32 = jnp.float32
    count_blocks, stored, tile, _ = hamiltonian.shape
    rows, vecs = start_basis.shape
    devices = lax.axis_size("row")
    nodes = lax.axis_size("node")
    row_scale = math.sqrt(rows * devices)

    core_pairs = [(i, i ^ 1) for i in range(devices)]
    chip_pairs = [(i, (i + (1 if i % 2 else -1)) % devices) for i in range(devices)]

    def halo(block):
        chip = lax.ppermute(block, "row", chip_pairs)
        core = lax.ppermute(block, "row", core_pairs)
        return core, chip

    modulus = node_re * node_re + node_im * node_im
    inverse_re = node_re / modulus
    inverse_im = -node_im / modulus
    power_re, power_im = inverse_re, inverse_im
    listed = []
    for degree in range(SWEEPS + 1):
        active = (sweep_count >= degree).astype(f32)
        listed.append((active * (weight_re * power_re - weight_im * power_im))[None, :])
        power_re, power_im = (
            power_re * inverse_re - power_im * inverse_im,
            power_re * inverse_im + power_im * inverse_re,
        )
    start_core, start_chip = halo(start_basis)
    wide = rows * 3
    high, low, odd, coef = call(
        functools.partial(prepare_kernel, count_blocks * devices),
        (
            jax.ShapeDtypeStruct((rows, wide), jnp.bfloat16),
            jax.ShapeDtypeStruct((rows, wide), jnp.bfloat16),
            jax.ShapeDtypeStruct((SUBLANES, 128), jnp.int32),
            jax.ShapeDtypeStruct((SUBLANES, 128), f32),
        ),
        2 + len(listed),
        smem=(0,),
        scratch=[pltpu.VMEM((count_blocks, 3 * count_blocks, tile, tile), f32)],
        flops=hamiltonian.size * 4,
        moved=hamiltonian.size * 4 + rows * wide * 8,
        name="prepare",
    )(column_blocks, *listed, hamiltonian)

    square = jax.ShapeDtypeStruct((rows, vecs), f32)

    def near(own):
        return call(
            near_kernel, square, 3,
            flops=12 * rows * rows * vecs, moved=8 * rows * rows + 12 * rows * vecs, name="near",
        )(high, low, own)

    first = call(
        sweep_kernel, square, 5,
        flops=6 * rows * rows * vecs, moved=4 * rows * rows + 12 * rows * vecs, name="sweep",
    )(high, low, start_basis, start_core, start_chip)
    first, coef = lax.optimization_barrier((first, coef))
    first_core, first_chip = halo(first)
    other = coef
    for shift in range(1, nodes):
        moved = lax.ppermute(coef, "node", [(i, i ^ shift) for i in range(nodes)])
        other = moved if shift == 1 else other + moved

    half = vecs // 2
    part = jax.ShapeDtypeStruct((half + SUBLANES, half), f32)
    filtered, mine, theirs = call(
        gram_kernel,
        (jax.ShapeDtypeStruct((rows, vecs), f32), part, part),
        10,
        flops=6 * rows * rows * vecs + 4 * rows * vecs * vecs,
        moved=rows * wide * 4 + 20 * rows * vecs,
        name="gram",
    )(high, low, first, near(first), first_core, first_chip, start_basis, coef, other, odd)

    total = mine + lax.ppermute(theirs, "row", core_pairs)
    steps = [1 << bit for bit in range(1, (devices - 1).bit_length())]
    phases = [[steps[0], steps[1], steps[0] + steps[1]]] if len(steps) > 1 else [steps]
    for phase in phases + [[step] for step in steps[2:]]:
        moved = [
            lax.ppermute(total, "row", [(i, i ^ step) for i in range(devices)]) for step in phase
        ]
        total = sum_up(total, moved)
    theirs = lax.ppermute(total, "row", core_pairs)

    return call(
        functools.partial(finish_kernel, row_scale),
        jax.ShapeDtypeStruct((rows, vecs), f32),
        4,
        out_any=True,
        scratch=[pltpu.VMEM((rows, vecs), f32), pltpu.SemaphoreType.DMA((2,))],
        flops=18 * vecs**3,
        moved=8 * rows * vecs + 4 * vecs * vecs,
        name="finish",
    )(filtered, total, theirs, odd)


def solution(mesh):
    return jax.shard_map(
        on_device,
        mesh=mesh,
        in_specs=(
            P("row", None, None, None),
            P("row", None),
            P("row", None),
            P("node"),
            P("node"),
            P("node"),
            P("node"),
            P("node"),
        ),
        out_specs=P("row", None),
        check_vma=False,
    )
```

```python
import functools
import math

import jax
import jax.numpy as jnp
from jax import lax
from jax.experimental import pallas as pl
from jax.experimental.pallas import tpu as pltpu
from jax.sharding import PartitionSpec as P

SWEEPS = 2
Z_POLY = (2.25, -2.4375, 1.6875, -0.5625, 0.0625)
SUBLANES = 8

VMEM = pl.BlockSpec(memory_space=pltpu.VMEM)
ANY = pl.BlockSpec(memory_space=pl.ANY)
SMEM = pl.BlockSpec(memory_space=pltpu.SMEM)


def split(x):
    high = x.astype(jnp.bfloat16)
    low = (x - high.astype(jnp.float32)).astype(jnp.bfloat16)
    return high, low


def mm(a, b, dims=((1,), (0,))):
    return lax.dot_general(a, b, (dims, ((), ())), preferred_element_type=jnp.float32)


def mm3(a_high, a_low, b_high, b_low):
    return mm(a_high, b_high) + (mm(a_high, b_low) + mm(a_low, b_high))


def prepare_kernel(total_blocks, cols_ref, *refs):
    shares, (ham_ref, high_ref, low_ref, odd_ref, coef_ref, wide) = refs[:-6], refs[-6:]
    row = lax.broadcasted_iota(jnp.int32, coef_ref.shape, 0)
    coef = jnp.zeros(coef_ref.shape, jnp.float32)
    for degree, share in enumerate(shares):
        coef = jnp.where(row == degree, jnp.sum(share[...], axis=1, keepdims=True), coef)
    coef_ref[...] = coef
    count_blocks, stored, tile, _ = ham_ref.shape
    first = cols_ref[0, 0]
    odd = (first // count_blocks) % 2
    odd_ref[...] = jnp.full(odd_ref.shape, odd, jnp.int32)
    wide[...] = jnp.zeros_like(wide)
    for block in range(count_blocks):
        for k in range(stored):
            away = lax.rem(cols_ref[block, k] - first + total_blocks, total_blocks)
            own = away < count_blocks
            right = jnp.logical_and(away >= count_blocks, away < 2 * count_blocks)
            within = jnp.where(
                own, away, jnp.where(right, away - count_blocks, away - total_blocks + count_blocks)
            )
            group = jnp.where(own, 0, jnp.where(right == (odd == 0), 1, 2))
            slot = group * count_blocks + within
            wide[block, slot] += ham_ref[block, k]
    for block in range(count_blocks):
        for slot in range(wide.shape[1]):
            high, low = split(wide[block, slot])
            rows = slice(block * tile, (block + 1) * tile)
            lanes = slice(slot * tile, (slot + 1) * tile)
            high_ref[rows, lanes] = high
            low_ref[rows, lanes] = low


def banded(high_ref, low_ref, first, parts):
    rows = parts[0].shape[0]
    total = None
    for index, part in enumerate(parts, first):
        lanes = slice(index * rows, (index + 1) * rows)
        b_high, b_low = split(part[...])
        term = mm3(high_ref[:, lanes], low_ref[:, lanes], b_high, b_low)
        total = term if total is None else total + term
    return total


def near_kernel(high_ref, low_ref, own_ref, out_ref):
    out_ref[...] = banded(high_ref, low_ref, 0, (own_ref,))


def sweep_kernel(high_ref, low_ref, own_ref, core_ref, chip_ref, out_ref):
    out_ref[...] = banded(high_ref, low_ref, 0, (own_ref, core_ref, chip_ref))


def gram_piece(filtered, take_second, out_ref):
    half = out_ref.shape[1]
    one, two = filtered[:, :half], filtered[:, half:]
    x_high, x_low = split(jnp.where(take_second, two, one))
    y_high, y_low = split(jnp.where(take_second, one, two))
    high = jnp.concatenate([x_high, y_high], axis=1)
    low = jnp.concatenate([x_low, y_low], axis=1)
    rows = ((0,), (0,))
    both = mm(x_high, high, rows) + (mm(x_high, low, rows) + mm(x_low, high, rows))
    same, cross = both[:, :half], both[:, half:]
    row = lax.broadcasted_iota(jnp.int32, (half, half), 0)
    col = lax.broadcasted_iota(jnp.int32, (half, half), 1)
    out_ref[:half] = jnp.where(col >= row, same, cross)
    diagonal = jnp.sum(jnp.where(col == row, cross, 0.0), axis=0, keepdims=True)
    out_ref[half:] = jnp.broadcast_to(diagonal, (SUBLANES, half))


def filter_kernel(
    high_ref, low_ref, own_ref, near_ref, core_ref, chip_ref, start_ref, coef_ref, other_ref, odd_ref,
    filtered_ref, theirs_ref,
):
    second = near_ref[...] + banded(high_ref, low_ref, 1, (core_ref, chip_ref))
    coef = coef_ref[...] + other_ref[...]
    filtered = (
        coef[0:1, 0:1] * start_ref[...] + coef[1:2, 0:1] * own_ref[...] + coef[2:3, 0:1] * second
    )
    filtered_ref[...] = filtered
    gram_piece(filtered, odd_ref[0:1, 0:1] == 0, theirs_ref)


def mine_kernel(filtered_ref, odd_ref, mine_ref):
    gram_piece(filtered_ref[...], odd_ref[0:1, 0:1] == 1, mine_ref)


def finish_kernel(row_scale, filtered_ref, mine_ref, theirs_ref, odd_ref, out_ref, held, sems):
    half = mine_ref.shape[1]
    odd = odd_ref[0:1, 0:1] == 1
    mine, theirs = mine_ref[...], theirs_ref[...]
    one, two = jnp.where(odd, theirs, mine), jnp.where(odd, mine, theirs)
    diagonal = one[half:half + 1]
    one, two = one[:half], two[:half]
    row = lax.broadcasted_iota(jnp.int32, (half, half), 0)
    col = lax.broadcasted_iota(jnp.int32, (half, half), 1)
    one_turned, two_turned = one.T, two.T
    upper = jnp.where(col >= row, one, one_turned)
    lower = jnp.where(col >= row, two, two_turned)
    side = jnp.where(col < row, one, jnp.where(col > row, two_turned, diagonal))
    side_turned = jnp.where(col < row, two, jnp.where(col > row, one_turned, diagonal))
    gram = jnp.concatenate(
        [
            jnp.concatenate([upper, side], axis=1),
            jnp.concatenate([side_turned, lower], axis=1),
        ],
        axis=0,
    )
    g_high, g_low = split(gram)
    gram2 = mm3(g_high, g_low, g_high, g_low)
    squares = upper * upper + lower * lower + 2.0 * (side * side)
    square = jnp.sum(jnp.sum(squares, axis=0, keepdims=True), axis=1, keepdims=True)
    norm_value = jnp.sqrt(square + 1e-06)
    inverse = 1.0 / norm_value
    a = gram * inverse
    a2 = (gram2 * inverse) * inverse
    b_high, b_low = split(a2)
    c_high, c_low = split(Z_POLY[3] * a + Z_POLY[4] * a2)
    rest = Z_POLY[1] * a + Z_POLY[2] * a2 + mm3(b_high, b_low, c_high, c_low)
    scale = row_scale / jnp.sqrt(norm_value)
    z_high, z_low = split(rest)
    pieces = sems.shape[0]
    rows = out_ref.shape[0] // pieces
    copies = []
    for piece in range(pieces):
        part = pl.ds(piece * rows, rows)
        filtered = filtered_ref[part, :]
        f_high, f_low = split(filtered)
        held[part, :] = scale * (Z_POLY[0] * filtered + mm3(f_high, f_low, z_high, z_low))
        copy = pltpu.make_async_copy(held.at[part, :], out_ref.at[part, :], sems.at[piece])
        copy.start()
        copies.append(copy)
    for copy in copies:
        copy.wait()


def sum_up(total, moved):
    total = total + moved[0]
    if len(moved) == 3:
        total = total + (moved[1] + moved[2])
    return total


def call(kernel, out_shape, n_in, smem=(), out_any=False, scratch=(), flops=0, moved=0, name=None):
    n_out = len(out_shape) if isinstance(out_shape, (tuple, list)) else 1
    return pl.pallas_call(
        kernel,
        out_shape=out_shape,
        in_specs=[SMEM if i in smem else VMEM for i in range(n_in)],
        out_specs=[VMEM] * n_out if isinstance(out_shape, (tuple, list)) else ANY if out_any else VMEM,
        scratch_shapes=scratch,
        cost_estimate=pl.CostEstimate(flops=flops, bytes_accessed=moved, transcendentals=0),
        compiler_params=pltpu.CompilerParams(vmem_limit_bytes=24 * 2**20),
        name=name,
    )


def on_device(
    hamiltonian, column_blocks, start_basis, node_re, node_im, weight_re, weight_im, sweep_count
):
    f32 = jnp.float32
    count_blocks, stored, tile, _ = hamiltonian.shape
    rows, vecs = start_basis.shape
    devices = lax.axis_size("row")
    nodes = lax.axis_size("node")
    row_scale = math.sqrt(rows * devices)

    core_pairs = [(i, i ^ 1) for i in range(devices)]
    chip_pairs = [(i, (i + (1 if i % 2 else -1)) % devices) for i in range(devices)]

    def halo(block):
        chip = lax.ppermute(block, "row", chip_pairs)
        core = lax.ppermute(block, "row", core_pairs)
        return core, chip

    modulus = node_re * node_re + node_im * node_im
    inverse_re = node_re / modulus
    inverse_im = -node_im / modulus
    power_re, power_im = inverse_re, inverse_im
    listed = []
    for degree in range(SWEEPS + 1):
        active = (sweep_count >= degree).astype(f32)
        listed.append((active * (weight_re * power_re - weight_im * power_im))[None, :])
        power_re, power_im = (
            power_re * inverse_re - power_im * inverse_im,
            power_re * inverse_im + power_im * inverse_re,
        )
    start_core, start_chip = halo(start_basis)
    wide = rows * 3
    high, low, odd, coef = call(
        functools.partial(prepare_kernel, count_blocks * devices),
        (
            jax.ShapeDtypeStruct((rows, wide), jnp.bfloat16),
            jax.ShapeDtypeStruct((rows, wide), jnp.bfloat16),
            jax.ShapeDtypeStruct((SUBLANES, 128), jnp.int32),
            jax.ShapeDtypeStruct((SUBLANES, 128), f32),
        ),
        2 + len(listed),
        smem=(0,),
        scratch=[pltpu.VMEM((count_blocks, 3 * count_blocks, tile, tile), f32)],
        flops=hamiltonian.size * 4,
        moved=hamiltonian.size * 4 + rows * wide * 8,
        name="prepare",
    )(column_blocks, *listed, hamiltonian)

    square = jax.ShapeDtypeStruct((rows, vecs), f32)

    def near(own):
        return call(
            near_kernel, square, 3,
            flops=12 * rows * rows * vecs, moved=8 * rows * rows + 12 * rows * vecs, name="near",
        )(high, low, own)

    first = call(
        sweep_kernel, square, 5,
        flops=6 * rows * rows * vecs, moved=4 * rows * rows + 12 * rows * vecs, name="sweep",
    )(high, low, start_basis, start_core, start_chip)
    first, coef = lax.optimization_barrier((first, coef))
    first_core, first_chip = halo(first)
    other = coef
    for shift in range(1, nodes):
        moved = lax.ppermute(coef, "node", [(i, i ^ shift) for i in range(nodes)])
        other = moved if shift == 1 else other + moved

    half = vecs // 2
    part = jax.ShapeDtypeStruct((half + SUBLANES, half), f32)
    filtered, theirs = call(
        filter_kernel, (square, part), 10,
        flops=12 * rows * rows * vecs + 2 * rows * vecs * vecs,
        moved=rows * wide * 4 + 24 * rows * vecs, name="filter",
    )(high, low, first, near(first), first_core, first_chip, start_basis, coef, other, odd)
    swapped = lax.ppermute(theirs, "row", core_pairs)
    mine = call(
        mine_kernel, part, 2, flops=2 * rows * vecs * vecs, moved=6 * rows * vecs, name="mine"
    )(filtered, odd)
    total = mine + swapped
    steps = [1 << bit for bit in range(1, (devices - 1).bit_length())]
    phases = [[steps[0], steps[1], steps[0] + steps[1]]] if len(steps) > 1 else [steps]
    for phase in phases + [[step] for step in steps[2:]]:
        moved = [
            lax.ppermute(total, "row", [(i, i ^ step) for i in range(devices)]) for step in phase
        ]
        total = sum_up(total, moved)
    theirs = lax.ppermute(total, "row", core_pairs)

    return call(
        functools.partial(finish_kernel, row_scale),
        jax.ShapeDtypeStruct((rows, vecs), f32),
        4,
        out_any=True,
        scratch=[pltpu.VMEM((rows, vecs), f32), pltpu.SemaphoreType.DMA((2,))],
        flops=18 * vecs**3,
        moved=8 * rows * vecs + 4 * vecs * vecs,
        name="finish",
    )(filtered, total, theirs, odd)


def solution(mesh):
    return jax.shard_map(
        on_device,
        mesh=mesh,
        in_specs=(
            P("row", None, None, None),
            P("row", None),
            P("row", None),
            P("node"),
            P("node"),
            P("node"),
            P("node"),
            P("node"),
        ),
        out_specs=P("row", None),
        check_vma=False,
    )
```

```python
import functools
import math

import jax
import jax.numpy as jnp
from jax import lax
from jax.experimental import pallas as pl
from jax.experimental.pallas import tpu as pltpu
from jax.sharding import PartitionSpec as P

SWEEPS = 2
Z_POLY = (2.25, -2.4375, 1.6875, -0.5625, 0.0625)
SUBLANES = 8

VMEM = pl.BlockSpec(memory_space=pltpu.VMEM)
ANY = pl.BlockSpec(memory_space=pl.ANY)
SMEM = pl.BlockSpec(memory_space=pltpu.SMEM)


def split(x):
    high = x.astype(jnp.bfloat16)
    low = (x - high.astype(jnp.float32)).astype(jnp.bfloat16)
    return high, low


def mm(a, b, dims=((1,), (0,))):
    return lax.dot_general(a, b, (dims, ((), ())), preferred_element_type=jnp.float32)


def mm3(a_high, a_low, b_high, b_low):
    rows = a_high.shape[0]
    both = mm(jnp.concatenate([a_high, a_low], axis=0), b_high)
    return both[:rows] + (mm(a_high, b_low) + both[rows:])


def prepare_kernel(total_blocks, cols_ref, *refs):
    shares, (ham_ref, high_ref, low_ref, odd_ref, coef_ref, wide) = refs[:-6], refs[-6:]
    row = lax.broadcasted_iota(jnp.int32, coef_ref.shape, 0)
    coef = jnp.zeros(coef_ref.shape, jnp.float32)
    for degree, share in enumerate(shares):
        coef = jnp.where(row == degree, jnp.sum(share[...], axis=1, keepdims=True), coef)
    coef_ref[...] = coef
    count_blocks, stored, tile, _ = ham_ref.shape
    first = cols_ref[0, 0]
    odd = (first // count_blocks) % 2
    odd_ref[...] = jnp.full(odd_ref.shape, odd, jnp.int32)
    wide[...] = jnp.zeros_like(wide)
    for block in range(count_blocks):
        for k in range(stored):
            away = lax.rem(cols_ref[block, k] - first + total_blocks, total_blocks)
            own = away < count_blocks
            right = jnp.logical_and(away >= count_blocks, away < 2 * count_blocks)
            within = jnp.where(
                own, away, jnp.where(right, away - count_blocks, away - total_blocks + count_blocks)
            )
            group = jnp.where(own, 0, jnp.where(right == (odd == 0), 1, 2))
            slot = group * count_blocks + within
            wide[block, slot] += ham_ref[block, k]
    for block in range(count_blocks):
        for slot in range(wide.shape[1]):
            high, low = split(wide[block, slot])
            rows = slice(block * tile, (block + 1) * tile)
            lanes = slice(slot * tile, (slot + 1) * tile)
            high_ref[rows, lanes] = high
            low_ref[rows, lanes] = low


def banded(high_ref, low_ref, first, parts):
    rows = parts[0].shape[0]
    total = None
    for index, part in enumerate(parts, first):
        lanes = slice(index * rows, (index + 1) * rows)
        b_high, b_low = split(part[...])
        term = mm3(high_ref[:, lanes], low_ref[:, lanes], b_high, b_low)
        total = term if total is None else total + term
    return total


def near_kernel(high_ref, low_ref, own_ref, out_ref):
    out_ref[...] = banded(high_ref, low_ref, 0, (own_ref,))


def sweep_kernel(high_ref, low_ref, own_ref, core_ref, chip_ref, out_ref):
    out_ref[...] = banded(high_ref, low_ref, 0, (own_ref, core_ref, chip_ref))


def gram_kernel(
    high_ref, low_ref, own_ref, near_ref, core_ref, chip_ref, start_ref, coef_ref, other_ref, odd_ref,
    filtered_ref, mine_ref, theirs_ref,
):
    second = near_ref[...] + banded(high_ref, low_ref, 1, (core_ref, chip_ref))
    coef = coef_ref[...] + other_ref[...]
    filtered = (
        coef[0:1, 0:1] * start_ref[...] + coef[1:2, 0:1] * own_ref[...] + coef[2:3, 0:1] * second
    )
    filtered_ref[...] = filtered
    high, low = split(filtered)
    cross = mm(high, low, ((0,), (0,)))
    gram = mm(high, high, ((0,), (0,))) + (cross + cross.T)
    half = gram.shape[0] // 2
    row = lax.broadcasted_iota(jnp.int32, (half, half), 0)
    col = lax.broadcasted_iota(jnp.int32, (half, half), 1)
    upper, lower, side = gram[:half, :half], gram[half:, half:], gram[:half, half:]
    packed = jnp.where(col >= row, upper, lower)
    diagonal = jnp.sum(jnp.where(col == row, lower, 0.0), axis=0, keepdims=True)
    diagonal = jnp.broadcast_to(diagonal, (SUBLANES, half))
    odd = odd_ref[0:1, 0:1] == 1
    mine_ref[:half] = jnp.where(odd, packed, side)
    theirs_ref[:half] = jnp.where(odd, side, packed)
    mine_ref[half:] = diagonal
    theirs_ref[half:] = diagonal


def finish_kernel(row_scale, filtered_ref, mine_ref, theirs_ref, odd_ref, out_ref, held, sems):
    half = mine_ref.shape[1]
    odd = odd_ref[0:1, 0:1] == 1
    mine, theirs = mine_ref[...], theirs_ref[...]
    packed = jnp.where(odd, mine, theirs)
    side = jnp.where(odd, theirs, mine)[:half]
    diagonal = packed[half:half + 1]
    packed = packed[:half]
    row = lax.broadcasted_iota(jnp.int32, (half, half), 0)
    col = lax.broadcasted_iota(jnp.int32, (half, half), 1)
    turned = packed.T
    upper = jnp.where(col >= row, packed, turned)
    lower = jnp.where(col < row, packed, jnp.where(col > row, turned, diagonal))
    gram = jnp.concatenate(
        [
            jnp.concatenate([upper, side], axis=1),
            jnp.concatenate([side.T, lower], axis=1),
        ],
        axis=0,
    )
    g_high, g_low = split(gram)
    gram2 = mm3(g_high, g_low, g_high, g_low)
    squares = upper * upper + lower * lower + 2.0 * (side * side)
    square = jnp.sum(jnp.sum(squares, axis=0, keepdims=True), axis=1, keepdims=True)
    norm_value = jnp.sqrt(square + 1e-06)
    inverse = 1.0 / norm_value
    a = gram * inverse
    a2 = (gram2 * inverse) * inverse
    b_high, b_low = split(a2)
    c_high, c_low = split(Z_POLY[3] * a + Z_POLY[4] * a2)
    rest = Z_POLY[1] * a + Z_POLY[2] * a2 + mm3(b_high, b_low, c_high, c_low)
    scale = row_scale / jnp.sqrt(norm_value)
    z_high, z_low = split(rest)
    pieces = sems.shape[0]
    rows = out_ref.shape[0] // pieces
    copies = []
    for piece in range(pieces):
        part = pl.ds(piece * rows, rows)
        filtered = filtered_ref[part, :]
        f_high, f_low = split(filtered)
        held[part, :] = scale * (Z_POLY[0] * filtered + mm3(f_high, f_low, z_high, z_low))
        copy = pltpu.make_async_copy(held.at[part, :], out_ref.at[part, :], sems.at[piece])
        copy.start()
        copies.append(copy)
    for copy in copies:
        copy.wait()


def sum_up(total, moved):
    total = total + moved[0]
    if len(moved) == 3:
        total = total + (moved[1] + moved[2])
    return total


def call(kernel, out_shape, n_in, smem=(), out_any=False, scratch=(), flops=0, moved=0, name=None):
    n_out = len(out_shape) if isinstance(out_shape, (tuple, list)) else 1
    return pl.pallas_call(
        kernel,
        out_shape=out_shape,
        in_specs=[SMEM if i in smem else VMEM for i in range(n_in)],
        out_specs=[VMEM] * n_out if isinstance(out_shape, (tuple, list)) else ANY if out_any else VMEM,
        scratch_shapes=scratch,
        cost_estimate=pl.CostEstimate(flops=flops, bytes_accessed=moved, transcendentals=0),
        compiler_params=pltpu.CompilerParams(vmem_limit_bytes=24 * 2**20),
        name=name,
    )


def on_device(
    hamiltonian, column_blocks, start_basis, node_re, node_im, weight_re, weight_im, sweep_count
):
    f32 = jnp.float32
    count_blocks, stored, tile, _ = hamiltonian.shape
    rows, vecs = start_basis.shape
    devices = lax.axis_size("row")
    nodes = lax.axis_size("node")
    row_scale = math.sqrt(rows * devices)

    core_pairs = [(i, i ^ 1) for i in range(devices)]
    chip_pairs = [(i, (i + (1 if i % 2 else -1)) % devices) for i in range(devices)]

    def halo(block):
        chip = lax.ppermute(block, "row", chip_pairs)
        core = lax.ppermute(block, "row", core_pairs)
        return core, chip

    modulus = node_re * node_re + node_im * node_im
    inverse_re = node_re / modulus
    inverse_im = -node_im / modulus
    power_re, power_im = inverse_re, inverse_im
    listed = []
    for degree in range(SWEEPS + 1):
        active = (sweep_count >= degree).astype(f32)
        listed.append((active * (weight_re * power_re - weight_im * power_im))[None, :])
        power_re, power_im = (
            power_re * inverse_re - power_im * inverse_im,
            power_re * inverse_im + power_im * inverse_re,
        )
    start_core, start_chip = halo(start_basis)
    wide = rows * 3
    high, low, odd, coef = call(
        functools.partial(prepare_kernel, count_blocks * devices),
        (
            jax.ShapeDtypeStruct((rows, wide), jnp.bfloat16),
            jax.ShapeDtypeStruct((rows, wide), jnp.bfloat16),
            jax.ShapeDtypeStruct((SUBLANES, 128), jnp.int32),
            jax.ShapeDtypeStruct((SUBLANES, 128), f32),
        ),
        2 + len(listed),
        smem=(0,),
        scratch=[pltpu.VMEM((count_blocks, 3 * count_blocks, tile, tile), f32)],
        flops=hamiltonian.size * 4,
        moved=hamiltonian.size * 4 + rows * wide * 8,
        name="prepare",
    )(column_blocks, *listed, hamiltonian)

    square = jax.ShapeDtypeStruct((rows, vecs), f32)

    def near(own):
        return call(
            near_kernel, square, 3,
            flops=12 * rows * rows * vecs, moved=8 * rows * rows + 12 * rows * vecs, name="near",
        )(high, low, own)

    first = call(
        sweep_kernel, square, 5,
        flops=6 * rows * rows * vecs, moved=4 * rows * rows + 12 * rows * vecs, name="sweep",
    )(high, low, start_basis, start_core, start_chip)
    first, coef = lax.optimization_barrier((first, coef))
    first_core, first_chip = halo(first)
    other = coef
    for shift in range(1, nodes):
        moved = lax.ppermute(coef, "node", [(i, i ^ shift) for i in range(nodes)])
        other = moved if shift == 1 else other + moved

    half = vecs // 2
    part = jax.ShapeDtypeStruct((half + SUBLANES, half), f32)
    filtered, mine, theirs = call(
        gram_kernel,
        (jax.ShapeDtypeStruct((rows, vecs), f32), part, part),
        10,
        flops=6 * rows * rows * vecs + 4 * rows * vecs * vecs,
        moved=rows * wide * 4 + 20 * rows * vecs,
        name="gram",
    )(high, low, first, near(first), first_core, first_chip, start_basis, coef, other, odd)

    total = mine + lax.ppermute(theirs, "row", core_pairs)
    steps = [1 << bit for bit in range(1, (devices - 1).bit_length())]
    phases = [[steps[0], steps[1], steps[0] + steps[1]]] if len(steps) > 1 else [steps]
    for phase in phases + [[step] for step in steps[2:]]:
        moved = [
            lax.ppermute(total, "row", [(i, i ^ step) for i in range(devices)]) for step in phase
        ]
        total = sum_up(total, moved)
    theirs = lax.ppermute(total, "row", core_pairs)

    return call(
        functools.partial(finish_kernel, row_scale),
        jax.ShapeDtypeStruct((rows, vecs), f32),
        4,
        out_any=True,
        scratch=[pltpu.VMEM((rows, vecs), f32), pltpu.SemaphoreType.DMA((2,))],
        flops=18 * vecs**3,
        moved=8 * rows * vecs + 4 * vecs * vecs,
        name="finish",
    )(filtered, total, theirs, odd)


def solution(mesh):
    return jax.shard_map(
        on_device,
        mesh=mesh,
        in_specs=(
            P("row", None, None, None),
            P("row", None),
            P("row", None),
            P("node"),
            P("node"),
            P("node"),
            P("node"),
            P("node"),
        ),
        out_specs=P("row", None),
        check_vma=False,
    )
```
